512 devices in a mesh: tile: 64 (over z, y), win: 8 (over x, core).
Axes of the slice: x: 4, y: 8, z: 8, core: 2. Of those that a mesh axis runs over, the one named last changes fastest.
Arguments:
- spectra: bfloat16 [16, 512, 4096], P('win', 'tile'), may hold values from -6 to 6
- requests: int32 [64, 64, 2], P('tile'), may hold values from 0 to 7
- pair_first: int32 [16384], P('tile'), may hold values from 0 to 127
- pair_second: int32 [16384], P('tile'), may hold values from 0 to 127
- pair_count: int32 [64], P('tile'), may hold values from 1 to 256, 10240 in all
Outputs:
- correlations: float32 [16384, 1024], P(('tile', 'win'))
The draws below stay inside these ranges and needn't reach their ends.
Inputs may be any that keep to these rules, and one draw needn't show every extreme that they name: `pair_count`: some tile has all 256 pairs live.
All inputs are finite; a program needn't handle non-finite values. No bound on the sum of `pair_count` on one device may be relied on, other than what follows from the above.
Results may differ from the reference program's by a relative error of at most 0.0029.
Values may be sent and summed in bfloat16 or wider, within the bound.
No kernel may reach another device: no remote copies, remote signals or barrier semaphores. Data moves between devices by JAX's collectives and lax.ppermute only.
A program may use at most 64 MiB of HBM per device.

```python
import math
import jax
import jax.numpy as jnp
import numpy as np
from jax import lax

F = 2048
L = 1024
STA_DEV = 8
CAP = 2
PAIRS_DEV = 256
N_TILES = 64
STATIONS = 512
PAIRS = 16384
SLOTS = 128
HOURS = 16
N_TILE = 64


def set_ends(array, stream_key, low, high):
    dims = array.shape
    place = [jax.random.randint(jax.random.fold_in(stream_key, axis), (), 0, dims[axis]) for axis in range(len(dims))]
    array = array.at[tuple(place)].set(low)
    longest = dims.index(max(dims))
    place[longest] = (place[longest] + 1) % dims[longest]
    return array.at[tuple(place)].set(high)


def block_levels(rng, extent, shards, low, largest):
    loudness, own = 1.0, jax.random.fold_in(rng, 6)
    for axis_at, parts in shards:
        draws = jnp.exp(jax.random.uniform(jax.random.fold_in(own, axis_at), (parts,), jnp.float32, low / len(shards), largest / len(shards)))
        loudness = loudness * jnp.repeat(draws, extent[axis_at] // parts).reshape([-1 if axis == axis_at else 1 for axis in range(len(extent))])
    return loudness


def profile(amount, total, most, skew):
    weights = [(1 << 20) // math.isqrt(standing ** skew) + 1 for standing in range(2, amount + 1)]
    spare, holding = total - most - (amount - 1), [1] * (amount - 1)
    while spare > 0:
        candidates = [i for i in range(amount - 1) if holding[i] < most]
        mass, budget = sum([weights[i] for i in candidates]), spare
        for i in candidates:
            extra = min(most - holding[i], max(1, budget * weights[i] // mass), spare)
            holding[i] = holding[i] + extra
            spare = spare - extra
    return np.array([most] + holding)


def uneven_parts(own_key, count, total, bound, skew):
    if count == 2:
        one = jax.random.randint(own_key, (), max(1, total - bound), min(bound, total - 1) + 1)
        return jnp.stack([one, total - one])
    tallies = jnp.asarray(profile(count, total, bound, skew), jnp.int32)
    pairs = (count - 1) // 2
    donor, taker = tallies[1:1 + 2 * pairs:2], tallies[2:2 + 2 * pairs:2]
    room = jnp.minimum(donor - 1, bound - taker)
    moved = jax.random.randint(jax.random.fold_in(own_key, 1), (pairs,), 0, 1 << 20) % (room + 1)
    tallies = tallies.at[1:1 + 2 * pairs:2].set(donor - moved).at[2:2 + 2 * pairs:2].set(taker + moved)
    return tallies[jax.random.permutation(jax.random.fold_in(own_key, 2), count)]


def bell_draw(own_key, shape, scale, limit, shards=(), kind=jnp.bfloat16):
    loudness = block_levels(own_key, shape, shards, -0.22, 0.18) if shards else 1.0
    result = jax.random.normal(own_key, shape, jnp.float32) * scale * loudness
    return jnp.minimum(jnp.maximum(result, -limit), limit).astype(kind)


def setup_inputs(seed: int = 0) -> dict:
    arg_keys = jax.random.split(jax.random.key(seed), 6)
    return {
        "spectra": bell_draw(arg_keys[0], (HOURS, STATIONS, 2 * F), 1.0, 6.0, ((0, 8), (1, 64))),
        "requests": set_ends(jax.random.randint(arg_keys[1], (N_TILES, N_TILES, CAP), 0, STA_DEV), jax.random.fold_in(arg_keys[1], 1), 0, STA_DEV - 1).astype(jnp.int32),
        "pair_first": set_ends(jax.random.randint(arg_keys[2], (PAIRS,), 0, SLOTS), jax.random.fold_in(arg_keys[2], 1), 0, SLOTS - 1).astype(jnp.int32),
        "pair_second": set_ends(jax.random.randint(arg_keys[3], (PAIRS,), 0, SLOTS), jax.random.fold_in(arg_keys[3], 1), 0, SLOTS - 1).astype(jnp.int32),
        "pair_count": uneven_parts(arg_keys[4], N_TILES, N_TILE * PAIRS_DEV * 5 // 8, PAIRS_DEV, 2).astype(jnp.int32),
    }


def whiten(spectra):
    width = spectra.shape[-1] // 2
    values = spectra.astype(jnp.float32)
    real_part = values[..., :width]
    imag_part = values[..., width:]
    power = real_part * real_part + imag_part * imag_part
    level = lax.optimization_barrier(jnp.mean(power, axis=-1, keepdims=True))
    factor = lax.rsqrt(power + 0.1 * level + 1e-06)
    return jnp.concatenate([real_part * factor, imag_part * factor], axis=-1).astype(jnp.bfloat16)

def reference(spectra, requests, pair_first, pair_second, pair_count):
    whitened = whiten(spectra)
    scale = F / math.sqrt(F * HOURS)

    def per_tile(items):
        wanted, first, second, count = items
        homes = jnp.arange(N_TILE, dtype=jnp.int32)[:, None] * STA_DEV
        station_ids = (homes + wanted).reshape(-1).astype(jnp.int32)
        left = whitened[:, station_ids[first]].astype(jnp.float32)
        right = whitened[:, station_ids[second]].astype(jnp.float32)
        left_real, left_imag = (left[..., :F], left[..., F:])
        right_real, right_imag = (right[..., :F], right[..., F:])
        real_sum = lax.optimization_barrier(jnp.sum(left_real * right_real + left_imag * right_imag, axis=0))
        imag_sum = lax.optimization_barrier(jnp.sum(left_imag * right_real - left_real * right_imag, axis=0))
        live = (jnp.arange(PAIRS_DEV, dtype=jnp.int32) < count).astype(jnp.float32)[:, None]
        spectrum = lax.complex(real_sum * live, imag_sum * live)
        series = jnp.real(jnp.fft.ifft(spectrum, axis=-1)) * scale
        return jnp.concatenate([series[:, F - L // 2:], series[:, :L // 2]], axis=1)
    stacked = lax.map(per_tile, (requests, pair_first.reshape(N_TILE, PAIRS_DEV), pair_second.reshape(N_TILE, PAIRS_DEV), pair_count))
    return stacked.reshape(N_TILE * PAIRS_DEV, L)
```

```python
import math

import jax
import jax.numpy as jnp
import numpy as np
from jax import lax
from jax.experimental import pallas as pl
from jax.experimental.pallas import tpu as pltpu
from jax.sharding import PartitionSpec as P

LAGS = 1024
BINS = 2048
HALF = BINS // 2
LANES = 128
BLOCKS = HALF // LANES
ROWS = 4 * BLOCKS
VMEM_LIMIT = 48 * 1024 * 1024


def fold_table():
    lags = np.arange(LAGS, dtype=np.int64) - LAGS // 2
    turns = (np.arange(HALF, dtype=np.int64)[:, None] * lags[None, :]) % BINS
    angle = turns * (2.0 * math.pi / BINS)
    cosine, sine = np.cos(angle), -np.sin(angle)
    sign = 1.0 - 2.0 * (lags % 2)
    cosine[0] = (1.0 + sign) / 2
    sine[0] = (1.0 - sign) / 2
    return np.concatenate([cosine, sine]).astype(np.float32)


def whiten_kernel(wanted, spectra, send, blocks, white):
    hours, homes = spectra.shape[0], spectra.shape[1]
    values = spectra[...].reshape(hours * homes, 2 * BINS).astype(jnp.float32)
    real_part, imag_part = values[:, :BINS], values[:, BINS:]
    power = real_part * real_part + imag_part * imag_part
    level = jnp.mean(power, axis=-1, keepdims=True)
    factor = lax.rsqrt(power + 0.1 * level + 1e-06)
    row = lax.broadcasted_iota(jnp.int32, (2 * LANES, LANES), 0)
    column = lax.broadcasted_iota(jnp.int32, (2 * LANES, LANES), 1)
    mirror = jnp.where(row == LANES - column, 1.0, 0.0).astype(jnp.bfloat16)
    for part, base in ((real_part * factor, 0), (imag_part * factor, 2 * BLOCKS)):
        rounded = part.astype(jnp.bfloat16)
        for j in range(BLOCKS):
            blocks[:, base + j, :] = rounded[:, j * LANES : (j + 1) * LANES].astype(jnp.float32)
            near = 2 * BLOCKS - 1 - j
            head = near + 1 if j else BLOCKS
            pair = jnp.concatenate(
                [rounded[:, near * LANES : (near + 1) * LANES], rounded[:, head * LANES : (head + 1) * LANES]], axis=1
            )
            blocks[:, base + BLOCKS + j, :] = jnp.dot(pair, mirror, preferred_element_type=jnp.float32)
    white[...] = blocks[...].reshape(white.shape).astype(jnp.bfloat16)
    tiles, cap = send.shape[0], send.shape[1]

    @pl.loop(0, tiles, unroll=4)
    def _(tile):
        for c in range(cap):
            station = wanted[tile, c]
            for hour in range(hours):
                send[tile, c, hour] = white[hour, station]


def stack_kernel(first, second, count, slots, table, series, weights, sums, folded, sem):
    pairs, hours = sums.shape[0], slots.shape[1]
    load = pltpu.make_async_copy(table, weights, sem)
    load.start()
    place = lax.broadcasted_iota(jnp.int32, (BLOCKS, LANES), 0) + lax.broadcasted_iota(jnp.int32, (BLOCKS, LANES), 1)
    corner = place == 0

    @pl.loop(0, pairs, unroll=8)
    def _(p):
        a, b = first[p], second[p]
        total_real, total_imag = 0.0, 0.0
        for hour in range(hours):
            left = slots[a, hour].astype(jnp.float32)
            right = slots[b, hour].astype(jnp.float32)
            left_real, left_imag = left[: 2 * BLOCKS], left[2 * BLOCKS :]
            right_real, right_imag = right[: 2 * BLOCKS], right[2 * BLOCKS :]
            total_real = total_real + (left_real * right_real + left_imag * right_imag)
            total_imag = total_imag + (left_imag * right_real - left_real * right_imag)
        low, high = total_real[:BLOCKS], total_real[BLOCKS:]
        sums[p, :BLOCKS] = low + high
        sums[p, BLOCKS:] = jnp.where(corner, low - high, total_imag[:BLOCKS] - total_imag[BLOCKS:])

    live = lax.broadcasted_iota(jnp.int32, (pairs, LANES), 0) < count[0]
    for j in range(2 * BLOCKS):
        folded[:, j * LANES : (j + 1) * LANES] = jnp.where(live, sums[:, j, :], 0.0).astype(jnp.bfloat16)
    load.wait()
    for j in range(0, LAGS, 256):
        series[:, j : j + 256] = jnp.dot(
            folded[...], weights[:, j : j + 256], preferred_element_type=jnp.float32
        ).astype(jnp.bfloat16)


def body(spectra, requests, pair_first, pair_second, pair_count, table):
    hours, homes = spectra.shape[0], spectra.shape[1]
    tiles, cap = requests.shape[1], requests.shape[2]
    pairs = pair_first.shape[0]
    windows = lax.axis_size("win")
    wanted = lax.all_to_all(requests[0], "tile", 0, 0, tiled=True)
    vmem = pl.BlockSpec(memory_space=pltpu.VMEM)
    smem = pl.BlockSpec(memory_space=pltpu.SMEM)
    send = pl.pallas_call(
        whiten_kernel,
        out_shape=jax.ShapeDtypeStruct((tiles, cap, hours, ROWS, LANES), jnp.bfloat16),
        in_specs=[smem, vmem],
        out_specs=vmem,
        scratch_shapes=[
            pltpu.VMEM((hours * homes, ROWS, LANES), jnp.float32),
            pltpu.VMEM((hours, homes, ROWS, LANES), jnp.bfloat16),
        ],
        compiler_params=pltpu.CompilerParams(vmem_limit_bytes=VMEM_LIMIT),
    )(wanted, spectra)
    slots = lax.all_to_all(send, "tile", 0, 0, tiled=True).reshape(tiles * cap, hours, ROWS, LANES)
    series = pl.pallas_call(
        stack_kernel,
        out_shape=jax.ShapeDtypeStruct((pairs, LAGS), jnp.bfloat16),
        in_specs=[smem, smem, smem, vmem, pl.BlockSpec(memory_space=pl.ANY)],
        out_specs=vmem,
        scratch_shapes=[
            pltpu.VMEM((BINS, LAGS), jnp.bfloat16),
            pltpu.VMEM((pairs, 2 * BLOCKS, LANES), jnp.float32),
            pltpu.VMEM((pairs, BINS), jnp.bfloat16),
            pltpu.SemaphoreType.DMA,
        ],
        compiler_params=pltpu.CompilerParams(vmem_limit_bytes=VMEM_LIMIT),
    )(pair_first, pair_second, pair_count, slots, table)
    parts = lax.all_to_all(series.reshape(windows, pairs // windows, LAGS), "win", 0, 0, tiled=True)
    scale = 1.0 / math.sqrt(BINS * hours * windows)
    return jnp.sum(parts.astype(jnp.float32), axis=0) * scale


def solution(mesh):
    table = fold_table().astype(jnp.bfloat16)
    mapped = jax.shard_map(
        body,
        mesh=mesh,
        in_specs=(P("win", "tile", None), P("tile", None, None), P("tile"), P("tile"), P("tile"), P()),
        out_specs=P(("tile", "win"), None),
        check_vma=False,
    )

    def run(spectra, requests, pair_first, pair_second, pair_count):
        return mapped(spectra, requests, pair_first, pair_second, pair_count, jnp.asarray(table))

    return run
```

```python
import math

import jax
import jax.numpy as jnp
import numpy as np
from jax import lax
from jax.experimental import pallas as pl
from jax.experimental.pallas import tpu as pltpu
from jax.sharding import Mesh
from jax.sharding import PartitionSpec as P

LAGS = 1024
BINS = 2048
HALF = BINS // 2
LANES = 128
BLOCKS = HALF // LANES
ROWS = 4 * BLOCKS
AXES = ("z", "y", "x", "core")
VMEM_LIMIT = 48 * 1024 * 1024


def fold_table():
    lags = np.arange(LAGS, dtype=np.int64) - LAGS // 2
    turns = (np.arange(HALF, dtype=np.int64)[:, None] * lags[None, :]) % BINS
    angle = turns * (2.0 * math.pi / BINS)
    cosine, sine = np.cos(angle), -np.sin(angle)
    sign = 1.0 - 2.0 * (lags % 2)
    cosine[0] = (1.0 + sign) / 2
    sine[0] = (1.0 - sign) / 2
    return np.concatenate([cosine, sine]).astype(np.float32)


def whiten_kernel(spectra, send, blocks):
    hours, homes = spectra.shape[0], spectra.shape[1]
    values = spectra[...].reshape(hours * homes, 2 * BINS).astype(jnp.float32)
    real_part, imag_part = values[:, :BINS], values[:, BINS:]
    power = real_part * real_part + imag_part * imag_part
    level = jnp.mean(power, axis=-1, keepdims=True)
    factor = lax.rsqrt(power + 0.1 * level + 1e-06)
    row = lax.broadcasted_iota(jnp.int32, (2 * LANES, LANES), 0)
    column = lax.broadcasted_iota(jnp.int32, (2 * LANES, LANES), 1)
    mirror = jnp.where(row == LANES - column, 1.0, 0.0).astype(jnp.bfloat16)
    for part, base in ((real_part * factor, 0), (imag_part * factor, 2 * BLOCKS)):
        rounded = part.astype(jnp.bfloat16)
        for j in range(BLOCKS):
            blocks[:, base + j, :] = rounded[:, j * LANES : (j + 1) * LANES].astype(jnp.float32)
            near = 2 * BLOCKS - 1 - j
            head = near + 1 if j else BLOCKS
            pair = jnp.concatenate(
                [rounded[:, near * LANES : (near + 1) * LANES], rounded[:, head * LANES : (head + 1) * LANES]], axis=1
            )
            blocks[:, base + BLOCKS + j, :] = jnp.dot(pair, mirror, preferred_element_type=jnp.float32)
    for item in range(hours * homes):
        white = blocks[item].astype(jnp.bfloat16)
        for peer in range(send.shape[0]):
            send[peer, item] = white


def pick_kernel(wanted, place, held, send):
    peers, sources, cap, hours = send.shape[:4]
    homes = held.shape[1] // hours
    base, source_step = place[0], place[1]

    @pl.loop(0, peers)
    def _(peer):
        for source in range(sources):
            for c in range(cap):
                station = wanted[peer, base + source * source_step + c]
                for hour in range(hours):
                    send[peer, source, c, hour] = held[source, hour * homes + station]


def stack_kernel(first, second, count, slots, weights, series, sums, folded):
    pairs, hours = sums.shape[0], slots.shape[1]
    place = lax.broadcasted_iota(jnp.int32, (BLOCKS, LANES), 0) + lax.broadcasted_iota(jnp.int32, (BLOCKS, LANES), 1)
    corner = place == 0

    @pl.loop(0, pairs, unroll=8)
    def _(p):
        a, b = first[p], second[p]
        total_real, total_imag = 0.0, 0.0
        for hour in range(hours):
            left = slots[a, hour].astype(jnp.float32)
            right = slots[b, hour].astype(jnp.float32)
            left_real, left_imag = left[: 2 * BLOCKS], left[2 * BLOCKS :]
            right_real, right_imag = right[: 2 * BLOCKS], right[2 * BLOCKS :]
            total_real = total_real + (left_real * right_real + left_imag * right_imag)
            total_imag = total_imag + (left_imag * right_real - left_real * right_imag)
        low, high = total_real[:BLOCKS], total_real[BLOCKS:]
        sums[p, :BLOCKS] = low + high
        sums[p, BLOCKS:] = jnp.where(corner, low - high, total_imag[:BLOCKS] - total_imag[BLOCKS:])

    live = lax.broadcasted_iota(jnp.int32, (pairs, LANES), 0) < count[0]
    for j in range(2 * BLOCKS):
        folded[:, j * LANES : (j + 1) * LANES] = jnp.where(live, sums[:, j, :], 0.0).astype(jnp.bfloat16)
    for j in range(0, LAGS, 256):
        series[:, j : j + 256] = jnp.dot(
            folded[...], weights[:, j : j + 256], preferred_element_type=jnp.float32
        ).astype(jnp.bfloat16)


def grid_groups(depth, height, width, cores):
    def number(z, y, x, core):
        return ((z * height + y) * width + x) * cores + core

    def along_z(core):
        return [[number(z, y, x, core) for z in range(depth)] for y in range(height) for x in range(width)]

    def along_y(core):
        return [[number(z, y, x, core) for y in range(height)] for z in range(depth) for x in range(width)]

    return along_z(0) + along_y(1), along_y(0) + along_z(1)


def body(spectra, requests, pair_first, pair_second, pair_count, table):
    hours, homes = spectra.shape[0], spectra.shape[1]
    tiles, cap = requests.shape[1], requests.shape[2]
    pairs = pair_first.shape[0]
    depth, height, width, cores = (lax.axis_size(name) for name in AXES)
    side = depth
    windows = width * cores
    core = lax.axis_index("core")
    z, y = lax.axis_index("z"), lax.axis_index("y")
    stage_one, stage_two = grid_groups(depth, height, width, cores)
    vmem = pl.BlockSpec(memory_space=pltpu.VMEM)
    smem = pl.BlockSpec(memory_space=pltpu.SMEM)
    params = pltpu.CompilerParams(vmem_limit_bytes=VMEM_LIMIT)

    wanted = lax.all_gather(
        requests.reshape(1, tiles * cap), AXES, axis=0, axis_index_groups=stage_two, tiled=True
    )
    copies = pl.pallas_call(
        whiten_kernel,
        out_shape=jax.ShapeDtypeStruct((side, hours * homes, ROWS, LANES), jnp.bfloat16),
        in_specs=[vmem],
        out_specs=vmem,
        scratch_shapes=[pltpu.VMEM((hours * homes, ROWS, LANES), jnp.float32)],
        compiler_params=params,
    )(spectra)
    held = lax.all_to_all(copies, AXES, 0, 0, axis_index_groups=stage_one, tiled=True)
    first_core = core == 0
    place = jnp.stack(
        [
            jnp.where(first_core, y * cap, z * height * cap),
            jnp.where(first_core, height * cap, cap),
        ]
    )
    send = pl.pallas_call(
        pick_kernel,
        out_shape=jax.ShapeDtypeStruct((side, side, cap, hours, ROWS, LANES), jnp.bfloat16),
        in_specs=[smem, smem, vmem],
        out_specs=vmem,
        compiler_params=params,
    )(wanted, place, held)
    slots = lax.all_to_all(send, AXES, 0, 0, axis_index_groups=stage_two, tiled=True)

    def where_held(slot):
        home, c = slot // cap, slot % cap
        turned = ((home % height) * depth + home // height) * cap + c
        return jnp.where(first_core, turned, slot)

    series = pl.pallas_call(
        stack_kernel,
        out_shape=jax.ShapeDtypeStruct((pairs, LAGS), jnp.bfloat16),
        in_specs=[smem, smem, smem, vmem, vmem],
        out_specs=vmem,
        scratch_shapes=[
            pltpu.VMEM((pairs, 2 * BLOCKS, LANES), jnp.float32),
            pltpu.VMEM((pairs, BINS), jnp.bfloat16),
        ],
        compiler_params=params,
    )(where_held(pair_first), where_held(pair_second), pair_count, slots.reshape(tiles * cap, hours, ROWS, LANES), table)
    parts = lax.all_to_all(series.reshape(windows, pairs // windows, LAGS), ("x", "core"), 0, 0, tiled=True)
    scale = 1.0 / math.sqrt(BINS * hours * windows)
    return jnp.sum(parts.astype(jnp.float32), axis=0) * scale


def solution(mesh):
    table = fold_table().astype(jnp.bfloat16)
    devices = mesh.devices
    grid = Mesh(devices.reshape(8, 8, 4, 2), AXES)
    mapped = jax.shard_map(
        body,
        mesh=grid,
        in_specs=(P(("x", "core"), ("z", "y"), None), P(("z", "y"), None, None), P(("z", "y")), P(("z", "y")), P(("z", "y")), P()),
        out_specs=P(AXES, None),
        check_vma=False,
    )

    def run(spectra, requests, pair_first, pair_second, pair_count):
        return mapped(spectra, requests, pair_first, pair_second, pair_count, jnp.asarray(table))

    return run
```

```python
import math

import jax
import jax.numpy as jnp
import numpy as np
from jax import lax
from jax.experimental import pallas as pl
from jax.experimental.pallas import tpu as pltpu
from jax.sharding import Mesh
from jax.sharding import PartitionSpec as P

LAGS = 1024
BINS = 2048
HALF = BINS // 2
LANES = 128
BLOCKS = HALF // LANES
ROWS = 4 * BLOCKS
HOURS = 16
SCALE = 1.0 / math.sqrt(BINS * HOURS)
STEP = 4
SPARE = 4
AXES = ("z", "y", "x", "core")
VMEM_LIMIT = 48 * 1024 * 1024


def fold_table():
    lags = np.arange(LAGS, dtype=np.int64) - LAGS // 2
    turns = (np.arange(HALF, dtype=np.int64)[:, None] * lags[None, :]) % BINS
    angle = turns * (2.0 * math.pi / BINS)
    cosine, sine = np.cos(angle), -np.sin(angle)
    sign = 1.0 - 2.0 * (lags % 2)
    cosine[0] = (1.0 + sign) / 2
    sine[0] = (1.0 - sign) / 2
    return np.concatenate([cosine, sine]).astype(np.float32)


def whiten_kernel(spectra, send, blocks):
    hours, homes = spectra.shape[0], spectra.shape[1]
    values = spectra[...].reshape(hours * homes, 2 * BINS).astype(jnp.float32)
    real_part, imag_part = values[:, :BINS], values[:, BINS:]
    power = real_part * real_part + imag_part * imag_part
    level = jnp.mean(power, axis=-1, keepdims=True)
    factor = lax.rsqrt(power + 0.1 * level + 1e-06)
    row = lax.broadcasted_iota(jnp.int32, (2 * LANES, LANES), 0)
    column = lax.broadcasted_iota(jnp.int32, (2 * LANES, LANES), 1)
    mirror = jnp.where(row == LANES - column, 1.0, 0.0).astype(jnp.bfloat16)
    for part, base in ((real_part * factor, 0), (imag_part * factor, 2 * BLOCKS)):
        rounded = part.astype(jnp.bfloat16)
        for j in range(BLOCKS):
            blocks[:, base + j, :] = rounded[:, j * LANES : (j + 1) * LANES].astype(jnp.float32)
            near = 2 * BLOCKS - 1 - j
            head = near + 1 if j else BLOCKS
            pair = jnp.concatenate(
                [rounded[:, near * LANES : (near + 1) * LANES], rounded[:, head * LANES : (head + 1) * LANES]], axis=1
            )
            blocks[:, base + BLOCKS + j, :] = jnp.dot(pair, mirror, preferred_element_type=jnp.float32)
    for item in range(hours * homes):
        white = blocks[item].astype(jnp.bfloat16)
        for peer in range(send.shape[0]):
            send[peer, item] = white


def pick_kernel(wanted, place, pairs, held, send, where):
    peers, sources, cap, hours = send.shape[:4]
    homes = held.shape[1] // hours
    base, source_step = place[0], place[1]

    @pl.loop(0, peers)
    def _(peer):
        for source in range(sources):
            for c in range(cap):
                station = wanted[peer, base + source * source_step + c]
                for hour in range(hours):
                    send[peer, source, c, hour] = held[source, hour * homes + station]

    slot = pairs[...]
    high, low, c = slot // (peers * cap), (slot // cap) % peers, slot % cap
    turned = (low * sources + high) * cap + c
    is_slot = lax.broadcasted_iota(jnp.int32, slot.shape, 0) < slot.shape[0] - SPARE
    where[...] = jnp.where((place[2] == 1) & is_slot, turned, slot)


def stack_kernel(pairs, slots, table, series, weights, sums, sem):
    count, hours = sums.shape[0], slots.shape[1]
    load = pltpu.make_async_copy(table, weights, sem)
    load.start()
    place = lax.broadcasted_iota(jnp.int32, (BLOCKS, LANES), 0) + lax.broadcasted_iota(jnp.int32, (BLOCKS, LANES), 1)
    corner = place == 0

    @pl.loop(0, count, unroll=16)
    def _(p):
        a, b = pairs[p], pairs[count + p]
        total_real, total_imag = 0.0, 0.0
        for hour in range(hours):
            left = slots[a, hour].astype(jnp.float32)
            right = slots[b, hour].astype(jnp.float32)
            left_real, left_imag = left[: 2 * BLOCKS], left[2 * BLOCKS :]
            right_real, right_imag = right[: 2 * BLOCKS], right[2 * BLOCKS :]
            total_real = total_real + (left_real * right_real + left_imag * right_imag)
            total_imag = total_imag + (left_imag * right_real - left_real * right_imag)
        low, high = total_real[:BLOCKS], total_real[BLOCKS:]
        sums[p, :BLOCKS] = low + high
        sums[p, BLOCKS:] = jnp.where(corner, low - high, total_imag[:BLOCKS] - total_imag[BLOCKS:])

    live = lax.broadcasted_iota(jnp.int32, (count, LANES), 0) < pairs[2 * count]
    load.wait()
    total = None
    for j in range(0, 2 * BLOCKS, STEP):
        folded = jnp.concatenate(
            [jnp.where(live, sums[:, j + i, :], 0.0).astype(jnp.bfloat16) for i in range(STEP)], axis=1
        )
        part = jnp.dot(folded, weights[j * LANES : (j + STEP) * LANES, :], preferred_element_type=jnp.float32)
        total = part if total is None else total + part
    series[...] = (total * SCALE).astype(jnp.bfloat16)


def grid_groups(depth, height, width, cores):
    def number(z, y, x, core):
        return ((z * height + y) * width + x) * cores + core

    def along_z(core):
        return [[number(z, y, x, core) for z in range(depth)] for y in range(height) for x in range(width)]

    def along_y(core):
        return [[number(z, y, x, core) for y in range(height)] for z in range(depth) for x in range(width)]

    return along_z(0) + along_y(1), along_y(0) + along_z(1)


def body(spectra, requests, pair_first, pair_second, pair_count, table):
    hours, homes = spectra.shape[0], spectra.shape[1]
    tiles, cap = requests.shape[1], requests.shape[2]
    pairs = pair_first.shape[0]
    depth, height, width, cores = (lax.axis_size(name) for name in AXES)
    side = depth
    windows = width * cores
    core = lax.axis_index("core")
    z, y = lax.axis_index("z"), lax.axis_index("y")
    stage_one, stage_two = grid_groups(depth, height, width, cores)
    vmem = pl.BlockSpec(memory_space=pltpu.VMEM)
    smem = pl.BlockSpec(memory_space=pltpu.SMEM)
    params = pltpu.CompilerParams(vmem_limit_bytes=VMEM_LIMIT)

    spot = jnp.where(core == 0, y, z)
    row = lax.broadcasted_iota(jnp.int32, (side, tiles * cap), 0)
    own = jnp.where(row == spot, requests.reshape(1, tiles * cap), 0)
    wanted = lax.psum(own, AXES, axis_index_groups=stage_two)
    copies = pl.pallas_call(
        whiten_kernel,
        out_shape=jax.ShapeDtypeStruct((side, hours * homes, ROWS, LANES), jnp.bfloat16),
        in_specs=[vmem],
        out_specs=vmem,
        scratch_shapes=[pltpu.VMEM((hours * homes, ROWS, LANES), jnp.float32)],
        compiler_params=params,
    )(spectra)
    held = lax.all_to_all(copies, AXES, 0, 0, axis_index_groups=stage_one, tiled=True)
    first_core = core == 0
    place = jnp.stack(
        [
            jnp.where(first_core, y * cap, z * height * cap),
            jnp.where(first_core, height * cap, cap),
            jnp.where(first_core, 1, 0),
        ]
    )
    spare = jnp.broadcast_to(pair_count, (SPARE * LANES,))
    described = jnp.concatenate([pair_first, pair_second, spare]).reshape(-1, LANES)
    send, where = pl.pallas_call(
        pick_kernel,
        out_shape=(
            jax.ShapeDtypeStruct((side, side, cap, hours, ROWS, LANES), jnp.bfloat16),
            jax.ShapeDtypeStruct(described.shape, jnp.int32),
        ),
        in_specs=[smem, smem, vmem, vmem],
        out_specs=(vmem, vmem),
        compiler_params=params,
    )(wanted, place, described, held)
    slots = lax.all_to_all(send, AXES, 0, 0, axis_index_groups=stage_two, tiled=True)
    series = pl.pallas_call(
        stack_kernel,
        out_shape=jax.ShapeDtypeStruct((pairs, LAGS), jnp.bfloat16),
        in_specs=[smem, vmem, pl.BlockSpec(memory_space=pl.ANY)],
        out_specs=vmem,
        scratch_shapes=[
            pltpu.VMEM((BINS, LAGS), jnp.bfloat16),
            pltpu.VMEM((pairs, 2 * BLOCKS, LANES), jnp.float32),
            pltpu.SemaphoreType.DMA,
        ],
        compiler_params=params,
    )(where.reshape(-1), slots.reshape(tiles * cap, hours, ROWS, LANES), table)
    parts = lax.all_to_all(series.reshape(windows, pairs // windows, LAGS), ("x", "core"), 0, 0, tiled=True)
    return jnp.sum(parts.astype(jnp.float32), axis=0)


def solution(mesh):
    table = fold_table().astype(jnp.bfloat16)
    devices = mesh.devices
    grid = Mesh(devices.reshape(8, 8, 4, 2), AXES)
    mapped = jax.shard_map(
        body,
        mesh=grid,
        in_specs=(P(("x", "core"), ("z", "y"), None), P(("z", "y"), None, None), P(("z", "y")), P(("z", "y")), P(("z", "y")), P()),
        out_specs=P(AXES, None),
        check_vma=False,
    )

    def run(spectra, requests, pair_first, pair_second, pair_count):
        return mapped(spectra, requests, pair_first, pair_second, pair_count, jnp.asarray(table))

    return run
```

```python
import math

import jax
import jax.numpy as jnp
import numpy as np
from jax import lax
from jax.experimental import pallas as pl
from jax.experimental.pallas import tpu as pltpu
from jax.sharding import Mesh
from jax.sharding import PartitionSpec as P

LAGS = 1024
BINS = 2048
HALF = BINS // 2
LANES = 128
BLOCKS = HALF // LANES
ROWS = 4 * BLOCKS
HOURS = 16
SCALE = 1.0 / math.sqrt(BINS * HOURS)
STEP = 2
SPARE = 4
AXES = ("z", "y", "x", "core")
VMEM_LIMIT = 16 * 1024 * 1024


def fold_table():
    lags = np.arange(LAGS, dtype=np.int64) - LAGS // 2
    turns = (np.arange(HALF, dtype=np.int64)[:, None] * lags[None, :]) % BINS
    angle = turns * (2.0 * math.pi / BINS)
    cosine, sine = np.cos(angle), -np.sin(angle)
    sign = 1.0 - 2.0 * (lags % 2)
    cosine[0] = (1.0 + sign) / 2
    sine[0] = (1.0 - sign) / 2
    return np.concatenate([cosine, sine]).astype(np.float32)


def whiten_kernel(spectra, send, blocks):
    hours, homes = spectra.shape[0], spectra.shape[1]
    values = spectra[...].reshape(hours * homes, 2 * BINS).astype(jnp.float32)
    real_part, imag_part = values[:, :BINS], values[:, BINS:]
    power = real_part * real_part + imag_part * imag_part
    level = jnp.mean(power, axis=-1, keepdims=True)
    factor = lax.rsqrt(power + 0.1 * level + 1e-06)
    row = lax.broadcasted_iota(jnp.int32, (2 * LANES, LANES), 0)
    column = lax.broadcasted_iota(jnp.int32, (2 * LANES, LANES), 1)
    mirror = jnp.where(row == LANES - column, 1.0, 0.0).astype(jnp.bfloat16)
    for part, base in ((real_part * factor, 0), (imag_part * factor, 2 * BLOCKS)):
        rounded = part.astype(jnp.bfloat16)
        for j in range(BLOCKS):
            blocks[:, base + j, :] = rounded[:, j * LANES : (j + 1) * LANES].astype(jnp.float32)
            near = 2 * BLOCKS - 1 - j
            head = near + 1 if j else BLOCKS
            pair = jnp.concatenate(
                [rounded[:, near * LANES : (near + 1) * LANES], rounded[:, head * LANES : (head + 1) * LANES]], axis=1
            )
            blocks[:, base + BLOCKS + j, :] = jnp.dot(pair, mirror, preferred_element_type=jnp.float32)
    for item in range(hours * homes):
        white = blocks[item].astype(jnp.bfloat16)
        for peer in range(send.shape[0]):
            send[peer, item] = white


def pick_kernel(wanted, place, pairs, held, send, where):
    peers, sources, cap, hours = send.shape[:4]
    homes = held.shape[1] // hours
    base, source_step = place[0], place[1]

    @pl.loop(0, peers, unroll=2)
    def _(peer):
        for source in range(sources):
            for c in range(cap):
                station = wanted[peer, c, base + source * source_step]
                for hour in range(hours):
                    send[peer, source, c, hour] = held[source, hour * homes + station]

    slot = pairs[...]
    high, low, c = slot // (peers * cap), (slot // cap) % peers, slot % cap
    turned = (low * sources + high) * cap + c
    is_slot = lax.broadcasted_iota(jnp.int32, slot.shape, 0) < slot.shape[0] - SPARE
    where[...] = jnp.where((place[2] == 1) & is_slot, turned, slot)


def stack_kernel(pairs, slots, weights, series, sums):
    count, hours = sums.shape[0], slots.shape[1]
    place = lax.broadcasted_iota(jnp.int32, (BLOCKS, LANES), 0) + lax.broadcasted_iota(jnp.int32, (BLOCKS, LANES), 1)
    corner = place == 0

    @pl.loop(0, count, unroll=16)
    def _(p):
        a, b = pairs[p], pairs[count + p]
        total_real, total_imag = 0.0, 0.0
        for hour in range(hours):
            left = slots[a, hour].astype(jnp.float32)
            right = slots[b, hour].astype(jnp.float32)
            left_real, left_imag = left[: 2 * BLOCKS], left[2 * BLOCKS :]
            right_real, right_imag = right[: 2 * BLOCKS], right[2 * BLOCKS :]
            total_real = total_real + (left_real * right_real + left_imag * right_imag)
            total_imag = total_imag + (left_imag * right_real - left_real * right_imag)
        low, high = total_real[:BLOCKS], total_real[BLOCKS:]
        sums[p, :BLOCKS] = low + high
        sums[p, BLOCKS:] = jnp.where(corner, low - high, total_imag[:BLOCKS] - total_imag[BLOCKS:])

    live = lax.broadcasted_iota(jnp.int32, (count, LANES), 0) < pairs[2 * count]
    total = None
    for j in range(0, 2 * BLOCKS, STEP):
        folded = jnp.concatenate(
            [jnp.where(live, sums[:, j + i, :], 0.0).astype(jnp.bfloat16) for i in range(STEP)], axis=1
        )
        part = jnp.dot(folded, weights[j * LANES : (j + STEP) * LANES, :], preferred_element_type=jnp.float32)
        total = part if total is None else total + part
    series[...] = (total * SCALE).astype(jnp.bfloat16)


def grid_groups(depth, height, width, cores):
    def number(z, y, x, core):
        return ((z * height + y) * width + x) * cores + core

    def along_z(core):
        return [[number(z, y, x, core) for z in range(depth)] for y in range(height) for x in range(width)]

    def along_y(core):
        return [[number(z, y, x, core) for y in range(height)] for z in range(depth) for x in range(width)]

    return along_z(0) + along_y(1), along_y(0) + along_z(1)


def body(spectra, requests, pair_first, pair_second, pair_count, table):
    hours, homes = spectra.shape[0], spectra.shape[1]
    tiles, cap = requests.shape[1], requests.shape[2]
    pairs = pair_first.shape[0]
    depth, height, width, cores = (lax.axis_size(name) for name in AXES)
    side = depth
    windows = width * cores
    core = lax.axis_index("core")
    z, y = lax.axis_index("z"), lax.axis_index("y")
    stage_one, stage_two = grid_groups(depth, height, width, cores)
    vmem = pl.BlockSpec(memory_space=pltpu.VMEM)
    smem = pl.BlockSpec(memory_space=pltpu.SMEM)
    params = pltpu.CompilerParams(vmem_limit_bytes=VMEM_LIMIT)

    spot = jnp.where(core == 0, y, z)
    row = lax.broadcasted_iota(jnp.int32, (side, cap, tiles), 0)
    own = jnp.where(row == spot, jnp.transpose(requests, (0, 2, 1)), 0)
    wanted = lax.psum(own, AXES, axis_index_groups=stage_two)
    copies = pl.pallas_call(
        whiten_kernel,
        out_shape=jax.ShapeDtypeStruct((side, hours * homes, ROWS, LANES), jnp.bfloat16),
        in_specs=[vmem],
        out_specs=vmem,
        scratch_shapes=[pltpu.VMEM((hours * homes, ROWS, LANES), jnp.float32)],
        compiler_params=params,
    )(spectra)
    held = lax.all_to_all(copies, AXES, 0, 0, axis_index_groups=stage_one, tiled=True)
    first_core = core == 0
    place = jnp.stack(
        [
            jnp.where(first_core, y, z * height),
            jnp.where(first_core, height, 1),
            jnp.where(first_core, 1, 0),
        ]
    )
    spare = jnp.broadcast_to(pair_count, (SPARE * LANES,))
    described = jnp.concatenate([pair_first, pair_second, spare]).reshape(-1, LANES)
    send, where = pl.pallas_call(
        pick_kernel,
        out_shape=(
            jax.ShapeDtypeStruct((side, side, cap, hours, ROWS, LANES), jnp.bfloat16),
            jax.ShapeDtypeStruct(described.shape, jnp.int32),
        ),
        in_specs=[smem, smem, vmem, vmem],
        out_specs=(vmem, vmem),
        compiler_params=params,
    )(wanted, place, described, held)
    slots = lax.all_to_all(send, AXES, 0, 0, axis_index_groups=stage_two, tiled=True)
    series = pl.pallas_call(
        stack_kernel,
        out_shape=jax.ShapeDtypeStruct((pairs, LAGS), jnp.bfloat16),
        in_specs=[smem, vmem, vmem],
        out_specs=vmem,
        scratch_shapes=[pltpu.VMEM((pairs, 2 * BLOCKS, LANES), jnp.float32)],
        compiler_params=params,
    )(where.reshape(-1), slots.reshape(tiles * cap, hours, ROWS, LANES), table)
    parts = lax.all_to_all(series.reshape(windows, pairs // windows, LAGS), ("x", "core"), 0, 0, tiled=True)
    return jnp.sum(parts.astype(jnp.float32), axis=0)


def solution(mesh):
    table = fold_table().astype(jnp.bfloat16)
    devices = mesh.devices
    grid = Mesh(devices.reshape(8, 8, 4, 2), AXES)
    mapped = jax.shard_map(
        body,
        mesh=grid,
        in_specs=(P(("x", "core"), ("z", "y"), None), P(("z", "y"), None, None), P(("z", "y")), P(("z", "y")), P(("z", "y")), P()),
        out_specs=P(AXES, None),
        check_vma=False,
    )

    def run(spectra, requests, pair_first, pair_second, pair_count):
        return mapped(spectra, requests, pair_first, pair_second, pair_count, jnp.asarray(table))

    return run
```

```python
import math

import jax
import jax.numpy as jnp
import numpy as np
from jax import lax
from jax.experimental import pallas as pl
from jax.experimental.pallas import tpu as pltpu
from jax.sharding import Mesh
from jax.sharding import PartitionSpec as P

LAGS = 1024
BINS = 2048
HALF = BINS // 2
LANES = 128
BLOCKS = HALF // LANES
ROWS = 4 * BLOCKS
HOURS = 16
SCALE = 1.0 / math.sqrt(BINS * HOURS)
STEP = 2
SPARE = 4
AXES = ("z", "y", "x", "core")
VMEM_LIMIT = 16 * 1024 * 1024


def fold_table():
    lags = np.arange(LAGS, dtype=np.int64) - LAGS // 2
    turns = (np.arange(HALF, dtype=np.int64)[:, None] * lags[None, :]) % BINS
    angle = turns * (2.0 * math.pi / BINS)
    cosine, sine = np.cos(angle), -np.sin(angle)
    sign = 1.0 - 2.0 * (lags % 2)
    cosine[0] = (1.0 + sign) / 2
    sine[0] = (1.0 - sign) / 2
    return np.concatenate([cosine, sine]).astype(np.float32)


def whiten_kernel(spectra, send, blocks):
    hours, homes = spectra.shape[0], spectra.shape[1]
    values = spectra[...].reshape(hours * homes, 2 * BINS).astype(jnp.float32)
    real_part, imag_part = values[:, :BINS], values[:, BINS:]
    power = real_part * real_part + imag_part * imag_part
    level = jnp.mean(power, axis=-1, keepdims=True)
    factor = lax.rsqrt(power + 0.1 * level + 1e-06)
    row = lax.broadcasted_iota(jnp.int32, (2 * LANES, LANES), 0)
    column = lax.broadcasted_iota(jnp.int32, (2 * LANES, LANES), 1)
    mirror = jnp.where(row == LANES - column, 1.0, 0.0).astype(jnp.bfloat16)
    for part, base in ((real_part * factor, 0), (imag_part * factor, 2 * BLOCKS)):
        rounded = part.astype(jnp.bfloat16)
        for j in range(BLOCKS):
            blocks[:, base + j, :] = rounded[:, j * LANES : (j + 1) * LANES].astype(jnp.float32)
            near = 2 * BLOCKS - 1 - j
            head = near + 1 if j else BLOCKS
            pair = jnp.concatenate(
                [rounded[:, near * LANES : (near + 1) * LANES], rounded[:, head * LANES : (head + 1) * LANES]], axis=1
            )
            blocks[:, base + BLOCKS + j, :] = jnp.dot(pair, mirror, preferred_element_type=jnp.float32)
    for item in range(hours * homes):
        white = blocks[item].astype(jnp.bfloat16)
        for peer in range(send.shape[0]):
            send[peer, item] = white


def pick_kernel(wanted, pairs, held, send, where):
    peers, sources, cap, hours = send.shape[:4]
    homes = held.shape[1] // hours
    first_core = lax.axis_index("core") == 0
    base = jnp.where(first_core, lax.axis_index("y"), lax.axis_index("z") * peers)
    source_step = jnp.where(first_core, peers, 1)

    for peer in range(peers):
        for source in range(sources):
            for c in range(cap):
                station = wanted[peer, c, base + source * source_step]
                for hour in range(hours):
                    send[peer, source, c, hour] = held[source, hour * homes + station]

    slot = pairs[...]
    high, low, c = slot // (peers * cap), (slot // cap) % peers, slot % cap
    turned = (low * sources + high) * cap + c
    is_slot = lax.broadcasted_iota(jnp.int32, slot.shape, 0) < slot.shape[0] - SPARE
    where[...] = jnp.where(first_core & is_slot, turned, slot)


def stack_kernel(pairs, slots, weights, series, sums):
    count, hours = sums.shape[0], slots.shape[1]
    place = lax.broadcasted_iota(jnp.int32, (BLOCKS, LANES), 0) + lax.broadcasted_iota(jnp.int32, (BLOCKS, LANES), 1)
    corner = place == 0

    @pl.loop(0, count, unroll=16)
    def _(p):
        a, b = pairs[p], pairs[count + p]
        total_real, total_imag = 0.0, 0.0
        for hour in range(hours):
            left = slots[a, hour].astype(jnp.float32)
            right = slots[b, hour].astype(jnp.float32)
            left_real, left_imag = left[: 2 * BLOCKS], left[2 * BLOCKS :]
            right_real, right_imag = right[: 2 * BLOCKS], right[2 * BLOCKS :]
            total_real = total_real + (left_real * right_real + left_imag * right_imag)
            total_imag = total_imag + (left_imag * right_real - left_real * right_imag)
        low, high = total_real[:BLOCKS], total_real[BLOCKS:]
        sums[p, :BLOCKS] = low + high
        sums[p, BLOCKS:] = jnp.where(corner, low - high, total_imag[:BLOCKS] - total_imag[BLOCKS:])

    live = lax.broadcasted_iota(jnp.int32, (count, LANES), 0) < pairs[2 * count]
    total = None
    for j in range(0, 2 * BLOCKS, STEP):
        folded = jnp.concatenate(
            [jnp.where(live, sums[:, j + i, :], 0.0).astype(jnp.bfloat16) for i in range(STEP)], axis=1
        )
        part = jnp.dot(folded, weights[j * LANES : (j + STEP) * LANES, :], preferred_element_type=jnp.float32)
        total = part if total is None else total + part
    series[...] = (total * SCALE).astype(jnp.bfloat16)


def grid_groups(depth, height, width, cores):
    def number(z, y, x, core):
        return ((z * height + y) * width + x) * cores + core

    def along_z(core):
        return [[number(z, y, x, core) for z in range(depth)] for y in range(height) for x in range(width)]

    def along_y(core):
        return [[number(z, y, x, core) for y in range(height)] for z in range(depth) for x in range(width)]

    return along_z(0) + along_y(1), along_y(0) + along_z(1)


def body(spectra, requests, pair_first, pair_second, pair_count, table):
    hours, homes = spectra.shape[0], spectra.shape[1]
    tiles, cap = requests.shape[1], requests.shape[2]
    pairs = pair_first.shape[0]
    depth, height, width, cores = (lax.axis_size(name) for name in AXES)
    side = depth
    windows = width * cores
    core = lax.axis_index("core")
    z, y = lax.axis_index("z"), lax.axis_index("y")
    stage_one, stage_two = grid_groups(depth, height, width, cores)
    vmem = pl.BlockSpec(memory_space=pltpu.VMEM)
    smem = pl.BlockSpec(memory_space=pltpu.SMEM)
    params = pltpu.CompilerParams(vmem_limit_bytes=VMEM_LIMIT)

    spot = jnp.where(core == 0, y, z)
    row = lax.broadcasted_iota(jnp.int32, (side, cap, tiles), 0)
    own = jnp.where(row == spot, jnp.transpose(requests, (0, 2, 1)), 0)
    wanted = lax.psum(own, AXES, axis_index_groups=stage_two)
    copies = pl.pallas_call(
        whiten_kernel,
        out_shape=jax.ShapeDtypeStruct((side, hours * homes, ROWS, LANES), jnp.bfloat16),
        in_specs=[vmem],
        out_specs=vmem,
        scratch_shapes=[pltpu.VMEM((hours * homes, ROWS, LANES), jnp.float32)],
        compiler_params=params,
    )(spectra)
    held = lax.all_to_all(copies, AXES, 0, 0, axis_index_groups=stage_one, tiled=True)
    spare = jnp.broadcast_to(pair_count, (SPARE * LANES,))
    described = jnp.concatenate([pair_first, pair_second, spare]).reshape(-1, LANES)
    send, where = pl.pallas_call(
        pick_kernel,
        out_shape=(
            jax.ShapeDtypeStruct((side, side, cap, hours, ROWS, LANES), jnp.bfloat16),
            jax.ShapeDtypeStruct(described.shape, jnp.int32),
        ),
        in_specs=[smem, vmem, vmem],
        out_specs=(vmem, vmem),
        compiler_params=params,
    )(wanted, described, held)
    slots = lax.all_to_all(send, AXES, 0, 0, axis_index_groups=stage_two, tiled=True)
    series = pl.pallas_call(
        stack_kernel,
        out_shape=jax.ShapeDtypeStruct((pairs, LAGS), jnp.bfloat16),
        in_specs=[smem, vmem, vmem],
        out_specs=vmem,
        scratch_shapes=[pltpu.VMEM((pairs, 2 * BLOCKS, LANES), jnp.float32)],
        compiler_params=params,
    )(where.reshape(-1), slots.reshape(tiles * cap, hours, ROWS, LANES), table)
    parts = lax.all_to_all(series.reshape(windows, pairs // windows, LAGS), ("x", "core"), 0, 0, tiled=True)
    return jnp.sum(parts.astype(jnp.float32), axis=0)


def solution(mesh):
    table = fold_table().astype(jnp.bfloat16)
    devices = mesh.devices
    grid = Mesh(devices.reshape(8, 8, 4, 2), AXES)
    mapped = jax.shard_map(
        body,
        mesh=grid,
        in_specs=(P(("x", "core"), ("z", "y"), None), P(("z", "y"), None, None), P(("z", "y")), P(("z", "y")), P(("z", "y")), P()),
        out_specs=P(AXES, None),
        check_vma=False,
    )

    def run(spectra, requests, pair_first, pair_second, pair_count):
        return mapped(spectra, requests, pair_first, pair_second, pair_count, jnp.asarray(table))

    return run
```

```python
import functools
import math

import jax
import jax.numpy as jnp
import numpy as np
from jax import lax
from jax.experimental import pallas as pl
from jax.experimental.pallas import tpu as pltpu
from jax.sharding import Mesh
from jax.sharding import PartitionSpec as P

LAGS = 1024
BINS = 2048
HALF = BINS // 2
LANES = 128
BLOCKS = HALF // LANES
ROWS = 4 * BLOCKS
HOURS = 16
SCALE = 1.0 / math.sqrt(BINS * HOURS)
STEP = 2
SPARE = 4
AXES = ("z", "y", "x", "core")
VMEM_LIMIT = 16 * 1024 * 1024


def fold_table():
    lags = np.arange(LAGS, dtype=np.int64) - LAGS // 2
    turns = (np.arange(HALF, dtype=np.int64)[:, None] * lags[None, :]) % BINS
    angle = turns * (2.0 * math.pi / BINS)
    cosine, sine = np.cos(angle), -np.sin(angle)
    sign = 1.0 - 2.0 * (lags % 2)
    cosine[0] = (1.0 + sign) / 2
    sine[0] = (1.0 - sign) / 2
    return np.concatenate([cosine, sine]).astype(np.float32)


def whiten_kernel(spectra, send, blocks):
    hours, homes = spectra.shape[0], spectra.shape[1]
    values = spectra[...].reshape(hours * homes, 2 * BINS).astype(jnp.float32)
    real_part, imag_part = values[:, :BINS], values[:, BINS:]
    power = real_part * real_part + imag_part * imag_part
    level = jnp.mean(power, axis=-1, keepdims=True)
    factor = lax.rsqrt(power + 0.1 * level + 1e-06)
    row = lax.broadcasted_iota(jnp.int32, (2 * LANES, LANES), 0)
    column = lax.broadcasted_iota(jnp.int32, (2 * LANES, LANES), 1)
    mirror = jnp.where(row == LANES - column, 1.0, 0.0).astype(jnp.bfloat16)
    for part, base in ((real_part * factor, 0), (imag_part * factor, 2 * BLOCKS)):
        rounded = part.astype(jnp.bfloat16)
        for j in range(BLOCKS):
            blocks[:, base + j, :] = rounded[:, j * LANES : (j + 1) * LANES].astype(jnp.float32)
            near = 2 * BLOCKS - 1 - j
            head = near + 1 if j else BLOCKS
            pair = jnp.concatenate(
                [rounded[:, near * LANES : (near + 1) * LANES], rounded[:, head * LANES : (head + 1) * LANES]], axis=1
            )
            blocks[:, base + BLOCKS + j, :] = jnp.dot(pair, mirror, preferred_element_type=jnp.float32)
    for item in range(hours * homes):
        white = blocks[item].astype(jnp.bfloat16)
        for peer in range(send.shape[0]):
            send[peer, item] = white


def pick_kernel(wanted, pairs, held, send, where):
    peers, sources, cap, hours = send.shape[:4]
    homes = held.shape[1] // hours
    first_core = lax.axis_index("core") == 0
    base = jnp.where(first_core, lax.axis_index("y"), lax.axis_index("z") * peers)
    source_step = jnp.where(first_core, peers, 1)

    for peer in range(peers):
        for source in range(sources):
            for c in range(cap):
                station = wanted[peer, c, base + source * source_step]
                for hour in range(hours):
                    send[peer, source, c, hour] = held[source, hour * homes + station]

    slot = pairs[...]
    high, low, c = slot // (peers * cap), (slot // cap) % peers, slot % cap
    turned = (low * sources + high) * cap + c
    is_slot = lax.broadcasted_iota(jnp.int32, slot.shape, 0) < slot.shape[0] - SPARE
    where[...] = jnp.where(first_core & is_slot, turned, slot)


def stack_kernel(owned, pairs, slots, weights, mine, theirs, sums):
    count, hours = sums.shape[0], slots.shape[1]
    place = lax.broadcasted_iota(jnp.int32, (BLOCKS, LANES), 0) + lax.broadcasted_iota(jnp.int32, (BLOCKS, LANES), 1)
    corner = place == 0

    @pl.loop(0, count, unroll=16)
    def _(p):
        a, b = pairs[p], pairs[count + p]
        total_real, total_imag = 0.0, 0.0
        for hour in range(hours):
            left = slots[a, hour].astype(jnp.float32)
            right = slots[b, hour].astype(jnp.float32)
            left_real, left_imag = left[: 2 * BLOCKS], left[2 * BLOCKS :]
            right_real, right_imag = right[: 2 * BLOCKS], right[2 * BLOCKS :]
            total_real = total_real + (left_real * right_real + left_imag * right_imag)
            total_imag = total_imag + (left_imag * right_real - left_real * right_imag)
        low, high = total_real[:BLOCKS], total_real[BLOCKS:]
        sums[p, :BLOCKS] = low + high
        sums[p, BLOCKS:] = jnp.where(corner, low - high, total_imag[:BLOCKS] - total_imag[BLOCKS:])

    live = lax.broadcasted_iota(jnp.int32, (count, LANES), 0) < pairs[2 * count]
    total = None
    for j in range(0, 2 * BLOCKS, STEP):
        folded = jnp.concatenate(
            [jnp.where(live, sums[:, j + i, :], 0.0).astype(jnp.bfloat16) for i in range(STEP)], axis=1
        )
        part = jnp.dot(folded, weights[j * LANES : (j + STEP) * LANES, :], preferred_element_type=jnp.float32)
        total = part if total is None else total + part
    total = total * SCALE
    core = lax.axis_index("core")
    for block in range(count // (2 * owned)):
        first = total[2 * block * owned : (2 * block + 1) * owned]
        second = total[(2 * block + 1) * owned : (2 * block + 2) * owned]
        rows = slice(block * owned, (block + 1) * owned)
        mine[rows] = jnp.where(core == 0, first, second)
        theirs[rows] = jnp.where(core == 0, second, first).astype(theirs.dtype)


def grid_groups(depth, height, width, cores):
    def number(z, y, x, core):
        return ((z * height + y) * width + x) * cores + core

    def along_z(core):
        return [[number(z, y, x, core) for z in range(depth)] for y in range(height) for x in range(width)]

    def along_y(core):
        return [[number(z, y, x, core) for y in range(height)] for z in range(depth) for x in range(width)]

    return along_z(0) + along_y(1), along_y(0) + along_z(1)


def body(spectra, requests, pair_first, pair_second, pair_count, table):
    hours, homes = spectra.shape[0], spectra.shape[1]
    tiles, cap = requests.shape[1], requests.shape[2]
    pairs = pair_first.shape[0]
    depth, height, width, cores = (lax.axis_size(name) for name in AXES)
    side = depth
    windows = width * cores
    core = lax.axis_index("core")
    z, y = lax.axis_index("z"), lax.axis_index("y")
    stage_one, stage_two = grid_groups(depth, height, width, cores)
    vmem = pl.BlockSpec(memory_space=pltpu.VMEM)
    smem = pl.BlockSpec(memory_space=pltpu.SMEM)
    params = pltpu.CompilerParams(vmem_limit_bytes=VMEM_LIMIT)

    spot = jnp.where(core == 0, y, z)
    row = lax.broadcasted_iota(jnp.int32, (side, cap, tiles), 0)
    own = jnp.where(row == spot, jnp.transpose(requests, (0, 2, 1)), 0)
    wanted = lax.psum(own, AXES, axis_index_groups=stage_two)
    copies = pl.pallas_call(
        whiten_kernel,
        out_shape=jax.ShapeDtypeStruct((side, hours * homes, ROWS, LANES), jnp.bfloat16),
        in_specs=[vmem],
        out_specs=vmem,
        scratch_shapes=[pltpu.VMEM((hours * homes, ROWS, LANES), jnp.float32)],
        compiler_params=params,
    )(spectra)
    held = lax.all_to_all(copies, AXES, 0, 0, axis_index_groups=stage_one, tiled=True)
    spare = jnp.broadcast_to(pair_count, (SPARE * LANES,))
    described = jnp.concatenate([pair_first, pair_second, spare]).reshape(-1, LANES)
    send, where = pl.pallas_call(
        pick_kernel,
        out_shape=(
            jax.ShapeDtypeStruct((side, side, cap, hours, ROWS, LANES), jnp.bfloat16),
            jax.ShapeDtypeStruct(described.shape, jnp.int32),
        ),
        in_specs=[smem, vmem, vmem],
        out_specs=(vmem, vmem),
        compiler_params=params,
    )(wanted, described, held)
    slots = lax.all_to_all(send, AXES, 0, 0, axis_index_groups=stage_two, tiled=True)
    owned = pairs // windows

    half = (pairs // cores, LAGS)
    ours, others = pl.pallas_call(
        functools.partial(stack_kernel, owned),
        out_shape=(jax.ShapeDtypeStruct(half, jnp.float32), jax.ShapeDtypeStruct(half, jnp.bfloat16)),
        in_specs=[smem, vmem, vmem],
        out_specs=(vmem, vmem),
        scratch_shapes=[pltpu.VMEM((pairs, 2 * BLOCKS, LANES), jnp.float32)],
        compiler_params=params,
    )(where.reshape(-1), slots.reshape(tiles * cap, hours, ROWS, LANES), table)
    theirs = lax.ppermute(others, "core", [(0, 1), (1, 0)])
    both = (ours + theirs.astype(jnp.float32)).astype(jnp.bfloat16)
    parts = lax.all_to_all(both.reshape(width, owned, LAGS), "x", 0, 0, tiled=True)
    return jnp.sum(parts.astype(jnp.float32), axis=0)


def solution(mesh):
    table = fold_table().astype(jnp.bfloat16)
    devices = mesh.devices
    grid = Mesh(devices.reshape(8, 8, 4, 2), AXES)
    mapped = jax.shard_map(
        body,
        mesh=grid,
        in_specs=(P(("x", "core"), ("z", "y"), None), P(("z", "y"), None, None), P(("z", "y")), P(("z", "y")), P(("z", "y")), P()),
        out_specs=P(AXES, None),
        check_vma=False,
    )

    def run(spectra, requests, pair_first, pair_second, pair_count):
        return mapped(spectra, requests, pair_first, pair_second, pair_count, jnp.asarray(table))

    return run
```

```python
import functools
import math

import jax
import jax.numpy as jnp
import numpy as np
from jax import lax
from jax.experimental import pallas as pl
from jax.experimental.pallas import tpu as pltpu
from jax.sharding import Mesh
from jax.sharding import PartitionSpec as P

LAGS = 1024
BINS = 2048
HALF = BINS // 2
LANES = 128
BLOCKS = HALF // LANES
ROWS = 4 * BLOCKS
HOURS = 16
SCALE = 1.0 / math.sqrt(BINS * HOURS)
STEP = 2
SPARE = 4
AXES = ("z", "y", "x", "core")
VMEM_LIMIT = 16 * 1024 * 1024


def fold_table():
    lags = np.arange(LAGS, dtype=np.int64) - LAGS // 2
    turns = (np.arange(HALF, dtype=np.int64)[:, None] * lags[None, :]) % BINS
    angle = turns * (2.0 * math.pi / BINS)
    cosine, sine = np.cos(angle), -np.sin(angle)
    sign = 1.0 - 2.0 * (lags % 2)
    cosine[0] = (1.0 + sign) / 2
    sine[0] = (1.0 - sign) / 2
    return np.concatenate([cosine, sine]).astype(np.float32)


def whiten_kernel(spectra, send, blocks):
    hours, homes = spectra.shape[0], spectra.shape[1]
    values = spectra[...].reshape(hours * homes, 2 * BINS).astype(jnp.float32)
    real_part, imag_part = values[:, :BINS], values[:, BINS:]
    power = real_part * real_part + imag_part * imag_part
    level = jnp.mean(power, axis=-1, keepdims=True)
    factor = lax.rsqrt(power + 0.1 * level + 1e-06)
    row = lax.broadcasted_iota(jnp.int32, (2 * LANES, LANES), 0)
    column = lax.broadcasted_iota(jnp.int32, (2 * LANES, LANES), 1)
    mirror = jnp.where(row == LANES - column, 1.0, 0.0).astype(jnp.bfloat16)
    for part, base in ((real_part * factor, 0), (imag_part * factor, 2 * BLOCKS)):
        rounded = part.astype(jnp.bfloat16)
        for j in range(BLOCKS):
            blocks[:, base + j, :] = rounded[:, j * LANES : (j + 1) * LANES].astype(jnp.float32)
            near = 2 * BLOCKS - 1 - j
            head = near + 1 if j else BLOCKS
            pair = jnp.concatenate(
                [rounded[:, near * LANES : (near + 1) * LANES], rounded[:, head * LANES : (head + 1) * LANES]], axis=1
            )
            blocks[:, base + BLOCKS + j, :] = jnp.dot(pair, mirror, preferred_element_type=jnp.float32)
    for item in range(hours * homes):
        white = blocks[item].astype(jnp.bfloat16)
        for peer in range(send.shape[0]):
            send[peer, item] = white


def pick_kernel(wanted, pairs, held, send, where):
    peers, sources, cap, hours = send.shape[:4]
    homes = held.shape[1] // hours
    first_core = lax.axis_index("core") == 0
    base = jnp.where(first_core, lax.axis_index("y"), lax.axis_index("z") * peers)
    source_step = jnp.where(first_core, peers, 1)

    for peer in range(peers):
        for source in range(sources):
            for c in range(cap):
                station = wanted[peer, c, base + source * source_step]
                for hour in range(hours):
                    send[peer, source, c, hour] = held[source, hour * homes + station]

    slot = pairs[...]
    high, low, c = slot // (peers * cap), (slot // cap) % peers, slot % cap
    turned = (low * sources + high) * cap + c
    is_slot = lax.broadcasted_iota(jnp.int32, slot.shape, 0) < slot.shape[0] - SPARE
    where[...] = jnp.where(first_core & is_slot, turned, slot)


def transform(owned, core, live, sums, weights):
    half = sums.shape[0] // 2
    starts = [pl.multiple_of(block * 2 * owned + core * owned, owned) for block in range(half // owned)]
    q = lax.broadcasted_iota(jnp.int32, (half, LANES), 0)
    is_live = (q // owned) * (2 * owned) + core * owned + q % owned < live

    def folded(j):
        rows = jnp.concatenate([sums[pl.ds(start, owned), j, :] for start in starts], axis=0)
        return jnp.where(is_live, rows, 0.0).astype(jnp.bfloat16)

    total = None
    for j in range(0, 2 * BLOCKS, STEP):
        block = jnp.concatenate([folded(j + i) for i in range(STEP)], axis=1)
        part = jnp.dot(block, weights[j * LANES : (j + STEP) * LANES, :], preferred_element_type=jnp.float32)
        total = part if total is None else total + part
    return total * SCALE


def stack_kernel(owned, pairs, slots, weights, theirs, sums):
    count, hours = sums.shape[0], slots.shape[1]
    core = lax.axis_index("core")
    place = lax.broadcasted_iota(jnp.int32, (BLOCKS, LANES), 0) + lax.broadcasted_iota(jnp.int32, (BLOCKS, LANES), 1)
    corner = place == 0

    @pl.loop(0, count, unroll=16)
    def _(p):
        a, b = pairs[p], pairs[count + p]
        total_real, total_imag = 0.0, 0.0
        for hour in range(hours):
            left = slots[a, hour].astype(jnp.float32)
            right = slots[b, hour].astype(jnp.float32)
            left_real, left_imag = left[: 2 * BLOCKS], left[2 * BLOCKS :]
            right_real, right_imag = right[: 2 * BLOCKS], right[2 * BLOCKS :]
            total_real = total_real + (left_real * right_real + left_imag * right_imag)
            total_imag = total_imag + (left_imag * right_real - left_real * right_imag)
        low, high = total_real[:BLOCKS], total_real[BLOCKS:]
        sums[p, :BLOCKS] = low + high
        sums[p, BLOCKS:] = jnp.where(corner, low - high, total_imag[:BLOCKS] - total_imag[BLOCKS:])

    theirs[...] = transform(owned, 1 - core, pairs[2 * count], sums, weights).astype(theirs.dtype)


def own_kernel(owned, pairs, sums, weights, mine):
    count = sums.shape[0]
    mine[...] = transform(owned, lax.axis_index("core"), pairs[2 * count], sums, weights)


def grid_groups(depth, height, width, cores):
    def number(z, y, x, core):
        return ((z * height + y) * width + x) * cores + core

    def along_z(core):
        return [[number(z, y, x, core) for z in range(depth)] for y in range(height) for x in range(width)]

    def along_y(core):
        return [[number(z, y, x, core) for y in range(height)] for z in range(depth) for x in range(width)]

    return along_z(0) + along_y(1), along_y(0) + along_z(1)


def body(spectra, requests, pair_first, pair_second, pair_count, table):
    hours, homes = spectra.shape[0], spectra.shape[1]
    tiles, cap = requests.shape[1], requests.shape[2]
    pairs = pair_first.shape[0]
    depth, height, width, cores = (lax.axis_size(name) for name in AXES)
    side = depth
    windows = width * cores
    core = lax.axis_index("core")
    z, y = lax.axis_index("z"), lax.axis_index("y")
    stage_one, stage_two = grid_groups(depth, height, width, cores)
    vmem = pl.BlockSpec(memory_space=pltpu.VMEM)
    smem = pl.BlockSpec(memory_space=pltpu.SMEM)
    params = pltpu.CompilerParams(vmem_limit_bytes=VMEM_LIMIT)

    spot = jnp.where(core == 0, y, z)
    row = lax.broadcasted_iota(jnp.int32, (side, cap, tiles), 0)
    own = jnp.where(row == spot, jnp.transpose(requests, (0, 2, 1)), 0)
    wanted = lax.psum(own, AXES, axis_index_groups=stage_two)
    copies = pl.pallas_call(
        whiten_kernel,
        out_shape=jax.ShapeDtypeStruct((side, hours * homes, ROWS, LANES), jnp.bfloat16),
        in_specs=[vmem],
        out_specs=vmem,
        scratch_shapes=[pltpu.VMEM((hours * homes, ROWS, LANES), jnp.float32)],
        compiler_params=params,
    )(spectra)
    held = lax.all_to_all(copies, AXES, 0, 0, axis_index_groups=stage_one, tiled=True)
    spare = jnp.broadcast_to(pair_count, (SPARE * LANES,))
    described = jnp.concatenate([pair_first, pair_second, spare]).reshape(-1, LANES)
    send, where = pl.pallas_call(
        pick_kernel,
        out_shape=(
            jax.ShapeDtypeStruct((side, side, cap, hours, ROWS, LANES), jnp.bfloat16),
            jax.ShapeDtypeStruct(described.shape, jnp.int32),
        ),
        in_specs=[smem, vmem, vmem],
        out_specs=(vmem, vmem),
        compiler_params=params,
    )(wanted, described, held)
    slots = lax.all_to_all(send, AXES, 0, 0, axis_index_groups=stage_two, tiled=True)
    owned = pairs // windows

    half = (pairs // cores, LAGS)
    others, sums = pl.pallas_call(
        functools.partial(stack_kernel, owned),
        out_shape=(jax.ShapeDtypeStruct(half, jnp.bfloat16), jax.ShapeDtypeStruct((pairs, 2 * BLOCKS, LANES), jnp.float32)),
        in_specs=[smem, vmem, vmem],
        out_specs=(vmem, vmem),
        compiler_params=params,
    )(where.reshape(-1), slots.reshape(tiles * cap, hours, ROWS, LANES), table)
    theirs = lax.ppermute(others, "core", [(0, 1), (1, 0)])
    ours = pl.pallas_call(
        functools.partial(own_kernel, owned),
        out_shape=jax.ShapeDtypeStruct(half, jnp.float32),
        in_specs=[smem, vmem, vmem],
        out_specs=vmem,
        compiler_params=params,
        cost_estimate=pl.CostEstimate(flops=550000000, bytes_accessed=5000000, transcendentals=0),
    )(where.reshape(-1), sums, table)
    both = (ours + theirs.astype(jnp.float32)).astype(jnp.bfloat16)
    parts = lax.all_to_all(both.reshape(width, owned, LAGS), "x", 0, 0, tiled=True)
    return jnp.sum(parts.astype(jnp.float32), axis=0)


def solution(mesh):
    table = fold_table().astype(jnp.bfloat16)
    devices = mesh.devices
    grid = Mesh(devices.reshape(8, 8, 4, 2), AXES)
    mapped = jax.shard_map(
        body,
        mesh=grid,
        in_specs=(P(("x", "core"), ("z", "y"), None), P(("z", "y"), None, None), P(("z", "y")), P(("z", "y")), P(("z", "y")), P()),
        out_specs=P(AXES, None),
        check_vma=False,
    )

    def run(spectra, requests, pair_first, pair_second, pair_count):
        return mapped(spectra, requests, pair_first, pair_second, pair_count, jnp.asarray(table))

    return run
```
